32 devices in a mesh: dp: 8 (over z, y), rep: 4 (over x, core).
Axes of the slice: x: 2, y: 2, z: 4, core: 2. Of those that a mesh axis runs over, the one named last changes fastest.
Arguments:
- tokens: bfloat16 [4096, 768], P(('dp', 'rep')), may hold values from -6 to 6
- seq_lengths: int32 [8, 3], P('dp'), may hold values from 0 to 512, as said below
- bucket_ids: int32 [1023], replicated, may hold values from 0 to 31
- routes: int32 [4096, 1], P(('dp', 'rep')), may hold values from 0 to 7; in each aligned block of 128 rows (0 to 127, 128 to 255, ...) at most 18 rows name the same one
- norm1_gain: bfloat16 [768], P('dp'), may hold values from 0.5 to 1.5
- w_query: bfloat16 [768, 768], P('dp'), may hold values from -0.21875 to 0.21875
- w_key: bfloat16 [768, 768], P('dp'), may hold values from -0.21875 to 0.21875
- w_value: bfloat16 [768, 768], P('dp'), may hold values from -0.21875 to 0.21875
- w_output: bfloat16 [768, 768], P('dp'), may hold values from -2.5 to 2.5
- rel_bias: bfloat16 [384], P('dp'), may hold values from -3 to 3
- norm2_gain: bfloat16 [768], P('dp'), may hold values from 0.5 to 1.5
- w_router: bfloat16 [768, 8], P('dp'), may hold values from -0.15625 to 0.15625
- w_in: bfloat16 [768, 24576], P(None, 'dp'), may hold values from -0.21875 to 0.21875
- w_out: bfloat16 [24576, 768], P('dp'), may hold values from -0.875 to 0.875
- cotangent: bfloat16 [4096, 768], P(('dp', 'rep')), may hold values from -6 to 6
Outputs:
- block_out: bfloat16 [4096, 768], P(('dp', 'rep'))
- grad_input: float32 [4096, 768], P(('dp', 'rep'))
- grad_norm1: float32 [768], P('dp')
- grad_query: float32 [768, 768], P('dp')
- grad_key: float32 [768, 768], P('dp')
- grad_value: float32 [768, 768], P('dp')
- grad_output: float32 [768, 768], P('dp')
- grad_rel_bias: float32 [384], P('dp')
- grad_norm2: float32 [768], P('dp')
- grad_router: float32 [768, 8], P('dp')
- grad_w_in: float32 [768, 24576], P(None, 'dp')
- grad_w_out: float32 [24576, 768], P('dp')
The draws below stay inside these ranges and needn't reach their ends.
Inputs may be any that keep to these rules, and one draw needn't show every extreme that they name: `seq_lengths`: row g lists the lengths of group g's sequences in order, then zeros; one to 3 are nonzero and they sum to at most 512. One sequence of each group starts in its first 128 places and ends in its last 128. `routes`: among one device's 128 tokens at most 18 name the same expert.
All inputs are finite; a program needn't handle non-finite values.
Results may differ from the reference program's by a relative error of at most 0.018.
Values may be sent and summed in bfloat16 or wider, within the bound.
A program may use at most 192 MiB of HBM per device.

```python
import math
import jax
import jax.numpy as jnp
import numpy as np
from jax import lax

D = 768
HEADS = 12
HEAD = 64
FF = 3072
BUCKETS = 32
EXPERTS = 8
MAXSEQ = 3
TOK_DEV = 128
CAP = 18
GROUP = 512
TOKENS = 4096
SPLIT = 1
FFS = 3072
N_DP = 8


def draw_seq_lengths(key, part):
    key = jax.random.fold_in(key, 7)
    key_list = jax.random.split(key, 5)
    seq_count = jax.random.randint(key_list[0], (N_DP,), 1, MAXSEQ + 1)
    long_slot = jax.random.randint(key_list[1], (N_DP,), 0, seq_count)
    shorts = jax.random.randint(key_list[2], (N_DP, MAXSEQ), 1, TOK_DEV // 2)
    slot_index = jnp.arange(MAXSEQ)[None, :]
    short_live = (slot_index < seq_count[:, None]) & (slot_index != long_slot[:, None])
    short_sum = jnp.sum(jnp.where(short_live, shorts, 0), axis=1)
    lowest = GROUP - TOK_DEV + 1
    highest = GROUP - short_sum
    long_len = lowest + jax.random.randint(key_list[3], (N_DP,), 0, highest - lowest + 1)
    lengths = jnp.where(slot_index == long_slot[:, None], long_len[:, None], jnp.where(short_live, shorts, 0))
    forced = jax.random.randint(key_list[4], (), 0, N_DP)
    whole_row = jnp.where(slot_index == 0, GROUP, 0)
    lengths = jnp.where(jnp.arange(N_DP)[:, None] == forced, whole_row, lengths)
    return lengths.astype(jnp.int32)


def set_ends(result, rng, low, high):
    shape = result.shape
    index_at = [jax.random.randint(jax.random.fold_in(rng, axis), (), 0, shape[axis]) for axis in range(len(shape))]
    result = result.at[tuple(index_at)].set(low)
    longest = shape.index(max(shape))
    index_at[longest] = (index_at[longest] + 1) % shape[longest]
    return result.at[tuple(index_at)].set(high)


def level_of(key, shape, pieces, smallest, high):
    def one(dim, parts):
        draws = jax.random.uniform(jax.random.fold_in(jax.random.fold_in(key, 6), dim), (parts,), jnp.float32, smallest / len(pieces), high / len(pieces))
        return jnp.repeat(jnp.exp(draws), shape[dim] // parts).reshape((-1,) + (1,) * (len(shape) - dim - 1))

    factor_of = one(*pieces[0])
    for cut in pieces[1:]:
        factor_of = factor_of * one(*cut)
    return factor_of


def shared_out(key, own, number, rows, number_of, top, bound, lean):
    ranking = jax.random.permutation(key, number_of)
    packed, ordinary = portions_of(number_of, rows * top, bound, lean, True), portions_of(number_of, rows * top, bound, lean, False)
    places = jnp.arange(number_of)

    def named(tallies, turn):
        used = int((tallies > 0).sum())
        fixed = max(1, used // 4)
        shifted = fixed + (places - fixed + turn * (used - fixed)) % max(1, number_of - fixed)
        return jnp.zeros((number_of,), jnp.int32).at[ranking[jnp.where(places < fixed, places, shifted)]].set(jnp.asarray(tallies, jnp.int32))

    tallies = jnp.where(number % 4 == 0, named(packed, number // 4), named(ordinary, number - number // 4 - 1))
    mixed = jax.random.permutation(jax.random.fold_in(own, 3), number_of)
    giver, receiver = mixed[0:number_of // 2 * 2:2], mixed[1:number_of // 2 * 2:2]
    margin = jnp.minimum(tallies[giver] - 1, bound - tallies[receiver]) // 2
    margin = jnp.where((giver == ranking[0]) | (receiver == ranking[0]) | (tallies[receiver] == 0), 0, jnp.maximum(margin, 0))
    shifted = jax.random.randint(jax.random.fold_in(own, 4), (number_of // 2,), 0, 1 << 20) % (margin + 1)
    tallies = tallies.at[giver].add(-shifted).at[receiver].add(shifted)
    items = jnp.searchsorted(jnp.cumsum(tallies), jnp.arange(rows * top), side="right").astype(jnp.int32)
    listing = items.reshape(top, rows).T
    listing = listing[jax.random.permutation(jax.random.fold_in(own, 1), rows)]
    turn = jax.random.randint(jax.random.fold_in(own, 2), (rows, 1), 0, top)
    return jnp.take_along_axis(listing, (jnp.arange(top)[None, :] + turn) % top, axis=1)


def portions_of(count, total, limit, lean, full):
    portions = [(1 << 20) // math.isqrt(grade ** lean) + 1 for grade in range(1, count + 1)]
    largest = limit if full else min(limit, max(-(-total // count), total * portions[0] // sum(portions)))
    least = 1 if total - largest >= count - 1 else 0
    holding, rest = [largest] + [least] * (count - 1), total - largest - least * (count - 1)
    while rest > 0:
        movable = [i for i in range(1, count) if holding[i] < largest] or [i for i in range(1, count) if holding[i] < limit]
        whole, budget = sum([portions[i] for i in movable]), rest
        for i in movable:
            addition = min(limit - holding[i], max(1, budget * portions[i] // whole), rest)
            holding[i] = holding[i] + addition
            rest = rest - addition
    return np.array(holding)


def normal_values(own_key, extent, spread, bound, pieces=(), held_as=jnp.bfloat16):
    gain = level_of(own_key, extent, pieces, -0.22, 0.18) if pieces else 1.0
    drawn = jax.random.normal(own_key, extent, jnp.float32) * spread * gain
    return jnp.minimum(jnp.maximum(drawn, -bound), bound).astype(held_as)


def setup_inputs(seed: int = 0) -> dict:
    keys = jax.random.split(jax.random.key(seed), 16)
    tokens = normal_values(keys[0], (TOKENS, D), 1.0, 6.0, ((0, 32),))
    seq_lengths = draw_seq_lengths(jax.random.fold_in(keys[15], 71), 0)
    bucket_ids = set_ends(jax.random.randint(keys[2], (2 * GROUP - 1,), 0, BUCKETS), jax.random.fold_in(keys[2], 1), 0, BUCKETS - 1).astype(jnp.int32)
    routes_keys = jax.random.split(jax.random.fold_in(keys[3], 1), TOKENS // TOK_DEV)
    routes_turns = jax.random.permutation(jax.random.fold_in(keys[3], 3), TOKENS // TOK_DEV)
    routes = jax.vmap(lambda own, number: shared_out(jax.random.fold_in(keys[3], 2), own, number, TOK_DEV, EXPERTS, 1, CAP, 2))(routes_keys, routes_turns).reshape((TOKENS, 1))
    norm1_gain = jnp.clip(1.0 + 0.1 * jax.random.normal(keys[4], (D,), jnp.float32), 0.5, 1.5).astype(jnp.bfloat16)
    w_query = normal_values(keys[5], (D, D), D ** -0.5, 0.21875, ((0, 8),))
    w_key = normal_values(keys[6], (D, D), D ** -0.5, 0.21875, ((0, 8),))
    w_value = normal_values(keys[7], (D, D), D ** -0.5, 0.21875, ((0, 8),))
    w_output = normal_values(keys[8], (D, D), (max(D // 128, 1)) ** -0.5, 2.5, ((0, 8),))
    rel_bias = normal_values(keys[9], (HEADS * BUCKETS,), 0.5, 3.0, ((0, 8),))
    norm2_gain = jnp.clip(1.0 + 0.1 * jax.random.normal(keys[10], (D,), jnp.float32), 0.5, 1.5).astype(jnp.bfloat16)
    w_router = normal_values(keys[11], (D, EXPERTS), (2 * D) ** -0.5, 0.15625, ((0, 8),))
    w_in = normal_values(keys[12], (D, EXPERTS * FF), D ** -0.5, 0.21875, ((1, 8),))
    w_out = normal_values(keys[13], (EXPERTS * FF, D), (max(FF // 64, 1)) ** -0.5, 0.875, ((0, 8),))
    cotangent = normal_values(keys[14], (TOKENS, D), 1.0, 6.0, ((0, 32),))
    return {"tokens": tokens, "seq_lengths": seq_lengths, "bucket_ids": bucket_ids, "routes": routes, "norm1_gain": norm1_gain, "w_query": w_query, "w_key": w_key, "w_value": w_value, "w_output": w_output, "rel_bias": rel_bias, "norm2_gain": norm2_gain, "w_router": w_router, "w_in": w_in, "w_out": w_out, "cotangent": cotangent}


@jax.custom_vjp
def low(v):
    return lax.optimization_barrier(v.astype(jnp.bfloat16)).astype(jnp.float32)

@jax.custom_vjp
def low_back(v):
    return v

def low_keep(v):
    return (low(v), None)

def low_pass(kept, grad):
    return (grad,)

def back_keep(v):
    return (v, None)

def back_low(kept, grad):
    return (low(grad),)
low.defvjp(low_keep, low_pass)
low_back.defvjp(back_keep, back_low)
EPS = 1e-06
NEG = -1e+30
HIGH = lax.Precision.HIGHEST

def rms_scale(rows_in, gain_vec):
    return rows_in * lax.rsqrt(lax.optimization_barrier(jnp.mean(rows_in * rows_in, axis=-1, keepdims=True)) + EPS) * gain_vec

def rounded(value):
    return low_back(low(value))

def layout(seq_lengths):
    seq_ends = jnp.cumsum(seq_lengths, axis=1).astype(jnp.int32)
    places = jnp.arange(GROUP, dtype=jnp.int32)
    segment = lax.optimization_barrier(jnp.sum((places[None, :, None] >= seq_ends[:, None, :]).astype(jnp.int32), axis=2)).astype(jnp.int32)
    is_valid = places[None, :] < seq_ends[:, -1:]
    return (segment, is_valid)

def bias_block(bias_flat, bucket_ids, first_row, row_count):
    bias_grid = bias_flat.reshape(HEADS, BUCKETS)
    bucket_onehot = (bucket_ids[None, :] == jnp.arange(BUCKETS, dtype=jnp.int32)[:, None]).astype(jnp.float32)
    by_offset = jnp.dot(bias_grid, bucket_onehot, precision=HIGH)
    query_at = first_row + jnp.arange(row_count, dtype=jnp.int32)
    offsets = query_at[:, None] - jnp.arange(GROUP, dtype=jnp.int32)[None, :] + (GROUP - 1)
    return by_offset[:, offsets]

def attend(inputs, rel_terms):
    q_group, k_group, v_group, segment = inputs
    q_heads = q_group.reshape(GROUP, HEADS, HEAD)
    k_heads = k_group.reshape(GROUP, HEADS, HEAD)
    v_heads = v_group.reshape(GROUP, HEADS, HEAD)
    raw_scores = low_back(jnp.einsum('qhd,khd->hqk', q_heads, k_heads, precision=HIGH) * HEAD ** (-0.5))
    allowed = segment[:, None] == segment[None, :]
    logit_sum = jnp.where(allowed[None], raw_scores + rel_terms, NEG)
    attend_probs = low(jax.nn.softmax(logit_sum, axis=-1))
    mixture = jnp.einsum('hqk,khd->qhd', attend_probs, v_heads, precision=HIGH)
    return mixture.reshape(GROUP, D)

def expert_slots(routes, valid_flat):
    device_count = TOKENS // TOK_DEV
    route_ids = routes[:, 0].reshape(device_count, TOK_DEV)
    row_live = valid_flat.reshape(device_count, TOK_DEV)
    chosen = (route_ids[:, :, None] == jnp.arange(EXPERTS, dtype=jnp.int32)[None, None, :]) & row_live[:, :, None]
    counts = jnp.cumsum(chosen.astype(jnp.int32), axis=1).astype(jnp.int32)
    rank_in = lax.optimization_barrier(jnp.sum(jnp.where(chosen, counts - 1, 0), axis=2)).astype(jnp.int32)
    device_ids = jnp.arange(device_count, dtype=jnp.int32)[:, None]
    place = (device_ids * CAP + rank_in).reshape(-1).astype(jnp.int32)
    target = jnp.where(row_live, route_ids, EXPERTS).reshape(-1).astype(jnp.int32)
    holder = jnp.zeros((EXPERTS, device_count * CAP), jnp.int32).at[target, place].set(jnp.arange(TOKENS, dtype=jnp.int32), mode='drop')
    slot_used = jnp.zeros((EXPERTS, device_count * CAP), jnp.float32).at[target, place].set(1.0, mode='drop')
    return (route_ids.reshape(-1), place, holder, slot_used)

def expert_pass(inputs, normed):
    w_first, w_second, token_ids, slot_used = inputs
    slot_rows = normed[token_ids] * slot_used[:, None]
    rows_split = low_back(jnp.broadcast_to(slot_rows[:, None, :], (slot_rows.shape[0], SPLIT, D)))
    hidden_pre = low_back(jnp.einsum('sjd,djf->sjf', rows_split, w_first.reshape(D, SPLIT, FFS), precision=HIGH))
    activation = low(jax.nn.gelu(hidden_pre, approximate=True))
    split_parts = jnp.einsum('sjf,jfd->sjd', activation, w_second.reshape(SPLIT, FFS, D), precision=HIGH)
    return lax.optimization_barrier(jnp.sum(low(split_parts), axis=1))

def reference(tokens, seq_lengths, bucket_ids, routes, norm1_gain, w_query, w_key, w_value, w_output, rel_bias, norm2_gain, w_router, w_in, w_out, cotangent):
    segment, is_valid = layout(seq_lengths)
    valid_flat = is_valid.reshape(-1)
    valid_rows = valid_flat.astype(jnp.float32)[:, None]
    route_ids, place, holder, slot_used = expert_slots(routes, valid_flat)
    route_onehot = (route_ids[:, None] == jnp.arange(EXPERTS, dtype=jnp.int32)[None, :]).astype(jnp.float32)

    def forward(x_in, gain_one, query_mat, key_mat, value_mat, output_mat, bias_flat, gain_two, router_mat, first_mat, second_mat):
        h_one = low(rms_scale(x_in, gain_one))
        q_all = rounded(jnp.dot(h_one, query_mat, precision=HIGH))
        k_all = rounded(jnp.dot(h_one, key_mat, precision=HIGH))
        v_all = rounded(jnp.dot(h_one, value_mat, precision=HIGH))
        rel_terms = bias_block(bias_flat, bucket_ids, 0, GROUP)

        def one_group(inputs):
            return attend(inputs, rel_terms)
        mixture = lax.map(jax.checkpoint(one_group), (q_all.reshape(N_DP, GROUP, D), k_all.reshape(N_DP, GROUP, D), v_all.reshape(N_DP, GROUP, D), segment))
        attn_mix = rounded(mixture.reshape(TOKENS, D))
        branch = low_back(jnp.dot(attn_mix, output_mat, precision=HIGH))
        x_one = x_in + valid_rows * branch
        h_two = low(rms_scale(x_one, gain_two))
        router_probs = jax.nn.softmax(jnp.dot(h_two, router_mat, precision=HIGH), axis=-1)
        gate_vals = lax.optimization_barrier(jnp.sum(router_probs * route_onehot, axis=1, keepdims=True))

        def one_expert(inputs):
            return expert_pass(inputs, h_two)
        slot_out = lax.map(jax.checkpoint(one_expert), (first_mat.reshape(D, EXPERTS, FF).transpose(1, 0, 2), second_mat.reshape(EXPERTS, FF, D), holder, slot_used))
        expert_rows = low_back(slot_out[route_ids, place] * valid_rows)
        return x_one + gate_vals * expert_rows * valid_rows
    block_out, pull_back = jax.vjp(forward, tokens.astype(jnp.float32), norm1_gain.astype(jnp.float32), w_query.astype(jnp.float32), w_key.astype(jnp.float32), w_value.astype(jnp.float32), w_output.astype(jnp.float32), rel_bias.astype(jnp.float32), norm2_gain.astype(jnp.float32), w_router.astype(jnp.float32), w_in.astype(jnp.float32), w_out.astype(jnp.float32))
    grads = pull_back(cotangent.astype(jnp.float32))
    return (block_out.astype(jnp.bfloat16), grads[0], grads[1], grads[2], grads[3], grads[4], grads[5], grads[6], grads[7], grads[8], grads[9], grads[10])
```

```python
import functools

import jax
import jax.numpy as jnp
from jax import lax
from jax.experimental import pallas as pl
from jax.experimental.pallas import tpu as pltpu
from jax.sharding import PartitionSpec as P

HEADS = 12
HEAD = 64
BUCKETS = 32
EXPERTS = 8


EPS = 1e-06
NEG = -1e30
HIGH = lax.Precision.HIGHEST
MESH = pl.DeviceIdType.MESH
VMEM_LIMIT = 48 * 1024 * 1024


def rms_scale(rows_in, gain_vec):
    return rows_in * lax.rsqrt(jnp.mean(rows_in * rows_in, axis=-1, keepdims=True) + EPS) * gain_vec


def matmul(left_op, right_op):
    return jnp.dot(left_op, right_op, preferred_element_type=jnp.float32)


def dot_over(left_op, right_op, left_dim, right_dim):
    return lax.dot_general(
        left_op, right_op, (((left_dim,), (right_dim,)), ((), ())), preferred_element_type=jnp.float32
    )


def exchange_kernel(jobs, sizes, in_count, *refs):
    ins, outs = refs[:in_count], refs[in_count : in_count + len(jobs)]
    sems = refs[in_count + len(jobs) :]
    axes = []
    for axis, _, _ in jobs:
        if axis not in axes:
            axes.append(axis)
    barrier = pltpu.get_barrier_semaphore()
    total = 0
    for axis in axes:
        me, count = lax.axis_index(axis), sizes[axis]
        for step in range(1, count):
            peer = lax.rem(me + step, count)
            pl.semaphore_signal(barrier, inc=1, device_id={axis: peer}, device_id_type=MESH)
        total += count - 1

    def local_and_remote(at, with_remote):
        axis, kind, source = jobs[at]
        me, count = lax.axis_index(axis), sizes[axis]
        from_ref = outs[source[1]] if isinstance(source, tuple) else ins[source]
        into_ref = outs[at]
        send, recv, own = sems[3 * at : 3 * at + 3]

        def part(peer):
            if kind == "gather":
                return from_ref
            if kind == "swap":
                return from_ref.at[peer]
            run = from_ref.shape[0] // count
            return from_ref.at[pl.ds(peer * run, run)]

        if not with_remote:
            return [pltpu.make_async_copy(part(me), into_ref.at[me], own)]
        found = []
        for step in range(1, count):
            peer = lax.rem(me + step, count)
            found.append(
                pltpu.make_async_remote_copy(
                    src_ref=part(peer),
                    dst_ref=into_ref.at[me],
                    send_sem=send.at[step - 1],
                    recv_sem=recv.at[step - 1],
                    device_id={axis: peer},
                    device_id_type=MESH,
                )
            )
        return found

    first = [at for at in range(len(jobs)) if not isinstance(jobs[at][2], tuple)]
    later = [at for at in range(len(jobs)) if isinstance(jobs[at][2], tuple)]
    flying = {at: local_and_remote(at, False) for at in first}
    for at in first:
        for copy in flying[at]:
            copy.start()
    pl.semaphore_wait(barrier, total)
    first.sort(key=lambda at: not any(jobs[other][2] == ("out", at) for other in later))
    for at in first:
        more = local_and_remote(at, True)
        for copy in more:
            copy.start()
        flying[at] += more
    for at in later:
        for copy in flying.pop(jobs[at][2][1]):
            copy.wait()
        flying[at] = local_and_remote(at, False) + local_and_remote(at, True)
        for copy in flying[at]:
            copy.start()
    for copies in flying.values():
        for copy in copies:
            copy.wait()


def exchange(mark, jobs, *arrays):
    sizes = {"dp": lax.axis_size("dp"), "rep": lax.axis_size("rep")}
    shapes = []
    for axis, kind, source in jobs:
        like = shapes[source[1]] if isinstance(source, tuple) else arrays[source]
        count = sizes[axis]
        if kind == "gather":
            shape = (count,) + tuple(like.shape)
        elif kind == "swap":
            shape = tuple(like.shape)
        else:
            shape = (count, like.shape[0] // count) + tuple(like.shape[1:])
        shapes.append(jax.ShapeDtypeStruct(shape, like.dtype))
    scratch = []
    for axis, _, _ in jobs:
        scratch += [
            pltpu.SemaphoreType.DMA((sizes[axis] - 1,)),
            pltpu.SemaphoreType.DMA((sizes[axis] - 1,)),
            pltpu.SemaphoreType.DMA,
        ]
    return pl.pallas_call(
        functools.partial(exchange_kernel, jobs, sizes, len(arrays)),
        out_shape=tuple(shapes),
        in_specs=[pl.BlockSpec(memory_space=pl.ANY)] * len(arrays),
        out_specs=tuple([pl.BlockSpec(memory_space=pl.ANY)] * len(jobs)),
        scratch_shapes=scratch,
        compiler_params=pltpu.CompilerParams(collective_id=mark, has_side_effects=True),
        name="exchange_%d" % mark,
    )(*arrays)


def attend_kernel(heads, block, qkv_ref, line_ref, seg_col_ref, seg_row_ref, probs_ref, mix_ref):
    rows = qkv_ref.shape[0]
    width = heads * HEAD
    for head in range(heads):
        low = head * HEAD
        k_head = qkv_ref[:, width + low : width + low + HEAD]
        v_head = qkv_ref[:, 2 * width + low : 2 * width + low + HEAD]
        line = line_ref[head : head + 1, :]
        span = line.shape[1]
        for start in range(0, rows, block):
            q_part = qkv_ref[start : start + block, low : low + HEAD]
            bias = pltpu.roll(
                jnp.broadcast_to(line, (block, span)), start, 1, stride=1, stride_axis=0
            )[:, :rows]
            scores = dot_over(q_part, k_head, 1, 1) * HEAD ** (-0.5) + bias
            allowed = seg_col_ref[start : start + block, :] == seg_row_ref[...]
            scores = jnp.where(allowed, scores, NEG)
            raised = jnp.exp(scores - jnp.max(scores, axis=-1, keepdims=True))
            probs = raised * (1.0 / jnp.sum(raised, axis=-1, keepdims=True))
            probs_ref[head, start : start + block, :] = probs
            mix_ref[start : start + block, low : low + HEAD] = matmul(
                probs.astype(jnp.bfloat16), v_head
            ).astype(jnp.bfloat16)


def attend(qkv, line, seg_col, seg_row, heads, block):
    rows = qkv.shape[0]
    return pl.pallas_call(
        functools.partial(attend_kernel, heads, block),
        out_shape=(
            jax.ShapeDtypeStruct((heads, rows, rows), jnp.float32),
            jax.ShapeDtypeStruct((rows, heads * HEAD), jnp.bfloat16),
        ),
        compiler_params=pltpu.CompilerParams(vmem_limit_bytes=VMEM_LIMIT),
        name="attend",
    )(qkv, line, seg_col, seg_row)


def attend_back_kernel(heads, block, qkv_ref, dmix_ref, probs_ref, dqkv_ref, dline_ref):
    rows = qkv_ref.shape[0]
    width = heads * HEAD
    span = dline_ref.shape[1]
    scale = HEAD ** (-0.5)
    for head in range(heads):
        low = head * HEAD
        k_head = qkv_ref[:, width + low : width + low + HEAD]
        v_head = qkv_ref[:, 2 * width + low : 2 * width + low + HEAD]
        dk = jnp.zeros((rows, HEAD), jnp.float32)
        dv = jnp.zeros((rows, HEAD), jnp.float32)
        dline = jnp.zeros((1, span), jnp.float32)
        for start in range(0, rows, block):
            q_part = qkv_ref[start : start + block, low : low + HEAD]
            dmix = dmix_ref[start : start + block, low : low + HEAD]
            probs = probs_ref[head, start : start + block, :]
            dprobs = dot_over(dmix, v_head, 1, 1)
            dscores = probs * (dprobs - jnp.sum(probs * dprobs, axis=-1, keepdims=True))
            low_scores = dscores.astype(jnp.bfloat16)
            dqkv_ref[start : start + block, low : low + HEAD] = (
                matmul(low_scores, k_head) * scale
            ).astype(jnp.bfloat16)
            dk = dk + dot_over(low_scores, q_part, 0, 0)
            dv = dv + dot_over(probs.astype(jnp.bfloat16), dmix, 0, 0)
            fold = jnp.concatenate(
                [dscores, jnp.zeros((block, span - rows), jnp.float32)], axis=1
            )
            half = block // 2
            while half >= 1:
                fold = fold[:half] + pltpu.roll(fold[half:], span - half, 1)
                half //= 2
            dline = dline + (pltpu.roll(fold, span - start, 1) if start else fold)
        dqkv_ref[:, width + low : width + low + HEAD] = (dk * scale).astype(jnp.bfloat16)
        dqkv_ref[:, 2 * width + low : 2 * width + low + HEAD] = dv.astype(jnp.bfloat16)
        dline_ref[head : head + 1, :] = dline


def attend_back(qkv, dmix, probs, heads, block):
    rows = qkv.shape[0]
    return pl.pallas_call(
        functools.partial(attend_back_kernel, heads, block),
        out_shape=(
            jax.ShapeDtypeStruct(qkv.shape, jnp.bfloat16),
            jax.ShapeDtypeStruct((heads, 2 * rows), jnp.float32),
        ),
        compiler_params=pltpu.CompilerParams(vmem_limit_bytes=VMEM_LIMIT),
        name="attend_back",
    )(qkv, dmix, probs)


def packed(parts, lead):
    flat = jnp.concatenate([piece.reshape(lead + (-1,)) for piece in parts], axis=-1)
    count = flat.shape[-1]
    whole = -(-count // 1024) * 1024
    flat = jnp.pad(flat, [(0, 0)] * len(lead) + [(0, whole - count)])
    return flat.reshape(lead + (whole // 128, 128))


def unpacked(flat, widths):
    found, at = [], 0
    for width in widths:
        found.append(flat[..., at : at + width])
        at += width
    return found


def local_columns(full, width, place):
    return lax.dynamic_slice_in_dim(full, place * width, width, axis=1)


def on_device(
    tokens,
    seq_lengths,
    bucket_ids,
    routes,
    norm1_gain,
    w_query,
    w_key,
    w_value,
    w_output,
    rel_bias,
    norm2_gain,
    w_router,
    w_in,
    w_out,
    cotangent,
):
    row_count, model_width = tokens.shape
    dp_count, rep_count = lax.axis_size("dp"), lax.axis_size("rep")
    rep_at = lax.axis_index("rep")
    group_rows = row_count * rep_count
    first_row = rep_at * row_count
    split_count = dp_count // EXPERTS
    capacity = row_count // 8 + row_count // 64
    heads = HEADS // rep_count
    width = heads * HEAD
    shard = w_query.shape[0]
    low_type = jnp.bfloat16

    piece_qkv = jnp.concatenate(
        [local_columns(full, width, rep_at) for full in (w_query, w_key, w_value)], axis=1
    )
    piece_out = local_columns(w_output, width, rep_at)
    small_widths = (shard, shard, rel_bias.shape[0], shard * EXPERTS)
    small = packed(
        [x.astype(jnp.float32) for x in (norm1_gain, norm2_gain, rel_bias, w_router)], ()
    )
    qkv_parts, out_parts, small_parts, token_parts, out_rows = exchange(
        1,
        (
            ("dp", "gather", 0),
            ("dp", "gather", 1),
            ("dp", "gather", 2),
            ("rep", "gather", 3),
            ("rep", "blocks", ("out", 1)),
        ),
        piece_qkv,
        piece_out,
        small,
        tokens,
    )
    w_qkv = qkv_parts.reshape(model_width, 3 * width)
    w_out_rows = (
        out_rows.reshape(rep_count, width, width).transpose(1, 0, 2).reshape(width, model_width)
    )
    gain_one, gain_two, table_flat, router_flat = unpacked(
        small_parts.reshape(dp_count, -1), small_widths
    )
    gain_first = gain_one.reshape(model_width)
    gain_second = gain_two.reshape(model_width)
    router_full = router_flat.reshape(model_width, EXPERTS).astype(low_type)
    table = lax.dynamic_slice_in_dim(table_flat.reshape(HEADS, BUCKETS), rep_at * heads, heads, 0)

    seq_ends = jnp.cumsum(seq_lengths[0])
    places = jnp.arange(group_rows, dtype=jnp.int32)
    segment = jnp.sum((places[:, None] >= seq_ends[None, :]).astype(jnp.int32), axis=1)
    live_bool = first_row + jnp.arange(row_count, dtype=jnp.int32) < seq_ends[-1]
    row_live = live_bool.astype(jnp.float32)[:, None]
    x_in = tokens.astype(jnp.float32)
    x_group = token_parts.reshape(group_rows, model_width).astype(jnp.float32)
    h_one = rms_scale(x_group, gain_first).astype(low_type)
    qkv = matmul(h_one, w_qkv).astype(low_type)

    by_step = jnp.concatenate(
        [
            bucket_ids[group_rows - 1 :: -1],
            jnp.full((1,), -1, jnp.int32),
            bucket_ids[: group_rows - 1 : -1],
        ]
    )
    bucket_hot = (by_step[None, :] == jnp.arange(BUCKETS, dtype=jnp.int32)[:, None]).astype(
        jnp.float32
    )
    line = jnp.dot(table, bucket_hot, precision=HIGH)
    probs, mixture = attend(qkv, line, segment[:, None], segment[None, :], heads, row_count)

    branch_parts = matmul(mixture, w_out_rows).astype(low_type)
    (branch_got,) = exchange(
        2,
        (("rep", "swap", 0),),
        branch_parts.reshape(rep_count, row_count, model_width),
    )
    branch = jnp.sum(branch_got.astype(jnp.float32), axis=0)
    x_one = x_in + row_live * branch
    h_two = rms_scale(x_one, gain_second).astype(low_type)
    router_probs = jax.nn.softmax(matmul(h_two, router_full), axis=-1)
    route_ids = routes[:, 0]
    route_onehot = route_ids[:, None] == jnp.arange(EXPERTS, dtype=jnp.int32)[None, :]
    gate_vals = jnp.sum(router_probs * route_onehot.astype(jnp.float32), axis=1, keepdims=True)
    chosen = route_onehot & live_bool[:, None]
    before = (
        jnp.arange(row_count, dtype=jnp.int32)[:, None]
        >= jnp.arange(row_count, dtype=jnp.int32)[None, :]
    ).astype(low_type)
    counts = matmul(before, chosen.astype(low_type)).astype(jnp.int32)
    rank_in = jnp.sum(jnp.where(chosen, counts - 1, 0), axis=1)
    slot_ids = jnp.where(live_bool, route_ids * capacity + rank_in, -1)
    slot_of = jnp.arange(dp_count * capacity, dtype=jnp.int32)
    slot_of = (slot_of // (capacity * split_count)) * capacity + slot_of % capacity
    dispatch = (slot_of[:, None] == slot_ids[None, :]).astype(low_type)

    grad_out = cotangent.astype(jnp.float32)
    grad_expert = (gate_vals * row_live * grad_out).astype(low_type)
    sent = matmul(dispatch, jnp.concatenate([h_two, grad_expert], axis=1)).astype(low_type)
    (got,) = exchange(
        3, (("dp", "swap", 0),), sent.reshape(dp_count, capacity, 2 * model_width)
    )
    got = got.reshape(dp_count * capacity, 2 * model_width)
    rows_here, grads_here = got[:, :model_width], got[:, model_width:]

    def expert(rows, grads):
        pre = matmul(rows, w_in)
        act, pull = jax.vjp(lambda inner: jax.nn.gelu(inner, approximate=True), pre)
        dpre = pull(dot_over(grads, w_out, 1, 1))[0]
        return act.astype(low_type), dpre.astype(low_type)

    act_here, dpre_here = expert(rows_here, grads_here)
    back = jnp.concatenate(
        [matmul(act_here, w_out).astype(low_type), dot_over(dpre_here, w_in, 1, 1).astype(low_type)],
        axis=1,
    )
    (returned,) = exchange(
        4, (("dp", "swap", 0),), back.reshape(dp_count, capacity, 2 * model_width)
    )
    landed = dot_over(dispatch, returned.reshape(dp_count * capacity, 2 * model_width), 0, 0)
    expert_rows, grad_h_two = landed[:, :model_width], landed[:, model_width:]

    block_out = x_one + gate_vals * expert_rows * row_live
    grad_gate = jnp.sum(grad_out * expert_rows, axis=1, keepdims=True) * row_live
    grad_probs = route_onehot.astype(jnp.float32) * grad_gate
    grad_logits = router_probs * (
        grad_probs - jnp.sum(router_probs * grad_probs, axis=1, keepdims=True)
    )
    grad_router = jnp.dot(h_two.astype(jnp.float32).T, grad_logits, precision=HIGH)
    grad_h_two = grad_h_two + jnp.dot(
        grad_logits, router_full.astype(jnp.float32).T, precision=HIGH
    )
    _, norm_two_pull = jax.vjp(rms_scale, x_one, gain_second)
    grad_x_norm, grad_gain_two = norm_two_pull(grad_h_two)
    grad_x_one = grad_out + grad_x_norm
    grad_branch = (grad_x_one * row_live).astype(low_type)

    branch_all, got_all = exchange(
        5, (("rep", "gather", 0), ("rep", "gather", 1)), grad_branch, got
    )
    grad_branch_group = branch_all.reshape(group_rows, model_width)
    grad_w_output = dot_over(mixture, grad_branch_group, 0, 0).astype(low_type)
    dmix = dot_over(grad_branch_group, w_out_rows, 1, 1).astype(low_type)
    dqkv, dline = attend_back(qkv, dmix, probs, heads, row_count)
    grad_table = jnp.dot(dline, bucket_hot.T, precision=HIGH)
    grad_w_qkv = dot_over(h_one, dqkv, 0, 0).astype(low_type)
    grad_h_parts = dot_over(dqkv, w_qkv, 1, 1).astype(low_type)
    grad_h_got, grad_out_cols = exchange(
        6,
        (("rep", "swap", 0), ("rep", "swap", 1)),
        grad_h_parts.reshape(rep_count, row_count, model_width),
        grad_w_output.reshape(width, rep_count, width).transpose(1, 0, 2),
    )
    grad_h_one = jnp.sum(grad_h_got.astype(jnp.float32), axis=0)
    _, norm_one_pull = jax.vjp(rms_scale, x_in, gain_first)
    grad_x_in, grad_gain_one = norm_one_pull(grad_h_one)
    grad_input = grad_x_one + grad_x_in

    table_whole = lax.dynamic_update_slice_in_dim(
        jnp.zeros((HEADS, BUCKETS), jnp.float32), grad_table, rep_at * heads, 0
    )
    small_grads = packed(
        [
            x.reshape(dp_count, -1)
            for x in (grad_gain_one, grad_gain_two, table_whole, grad_router)
        ],
        (dp_count,),
    )
    weight_got, out_got, small_got = exchange(
        7,
        (("dp", "swap", 0), ("dp", "swap", 1), ("dp", "swap", 2)),
        grad_w_qkv.reshape(dp_count, shard, 3 * width),
        grad_out_cols.reshape(dp_count, shard, width),
        small_grads,
    )
    weight_sum = jnp.concatenate(
        [
            jnp.sum(weight_got.astype(jnp.float32), axis=0),
            jnp.sum(out_got.astype(jnp.float32), axis=0),
        ],
        axis=1,
    ).astype(low_type)
    weight_all, small_all = exchange(
        8,
        (("rep", "gather", 0), ("rep", "gather", 1)),
        weight_sum,
        jnp.sum(small_got, axis=0),
    )
    weights = (
        weight_all.reshape(rep_count, shard, 4, width)
        .transpose(2, 1, 0, 3)
        .reshape(4, shard, model_width)
        .astype(jnp.float32)
    )
    small_sum = jnp.sum(small_all, axis=0).reshape(-1)
    out_gain_one, out_gain_two, out_table, out_router = unpacked(small_sum, small_widths)

    got_all = got_all.reshape(-1, 2 * model_width)
    rows_all, grads_all = got_all[:, :model_width], got_all[:, model_width:]
    act_all, dpre_all = expert(rows_all, grads_all)
    grad_w_in = dot_over(rows_all, dpre_all, 0, 0)
    grad_w_out = dot_over(act_all, grads_all, 0, 0)
    return (
        block_out.astype(low_type),
        grad_input,
        out_gain_one,
        weights[0],
        weights[1],
        weights[2],
        weights[3],
        out_table,
        out_gain_two,
        out_router.reshape(shard, EXPERTS),
        grad_w_in,
        grad_w_out,
    )


def solution(mesh):
    placed = (
        P(("dp", "rep"), None),
        P("dp", None),
        P(),
        P(("dp", "rep"), None),
        P("dp"),
        P("dp", None),
        P("dp", None),
        P("dp", None),
        P("dp", None),
        P("dp"),
        P("dp"),
        P("dp", None),
        P(None, "dp"),
        P("dp", None),
        P(("dp", "rep"), None),
    )
    return jax.shard_map(
        on_device,
        mesh=mesh,
        in_specs=placed,
        out_specs=(
            P(("dp", "rep"), None),
            P(("dp", "rep"), None),
            P("dp"),
            P("dp", None),
            P("dp", None),
            P("dp", None),
            P("dp", None),
            P("dp"),
            P("dp"),
            P("dp", None),
            P(None, "dp"),
            P("dp", None),
        ),
        check_vma=False,
    )
```

```python
import functools

import jax
import jax.numpy as jnp
from jax import lax
from jax.experimental import pallas as pl
from jax.experimental.pallas import tpu as pltpu
from jax.sharding import PartitionSpec as P

HEADS = 12
HEAD = 64
BUCKETS = 32
EXPERTS = 8


EPS = 1e-06
NEG = -1e30
HIGH = lax.Precision.HIGHEST
MESH = pl.DeviceIdType.MESH
VMEM_LIMIT = 48 * 1024 * 1024


def rms_scale(rows_in, gain_vec):
    return rows_in * lax.rsqrt(jnp.mean(rows_in * rows_in, axis=-1, keepdims=True) + EPS) * gain_vec


def matmul(left_op, right_op):
    return jnp.dot(left_op, right_op, preferred_element_type=jnp.float32)


def dot_over(left_op, right_op, left_dim, right_dim):
    return lax.dot_general(
        left_op, right_op, (((left_dim,), (right_dim,)), ((), ())), preferred_element_type=jnp.float32
    )


def exchange_kernel(jobs, sizes, in_count, *refs):
    ins, outs = refs[:in_count], refs[in_count : in_count + len(jobs)]
    sems = refs[in_count + len(jobs) :]
    axes = []
    for axis, _, _ in jobs:
        if axis not in axes:
            axes.append(axis)
    barrier = pltpu.get_barrier_semaphore()
    total = 0
    for axis in axes:
        me, count = lax.axis_index(axis), sizes[axis]
        for step in range(1, count):
            peer = lax.rem(me + step, count)
            pl.semaphore_signal(barrier, inc=1, device_id={axis: peer}, device_id_type=MESH)
        total += count - 1

    def local_and_remote(at, with_remote):
        axis, kind, source = jobs[at]
        me, count = lax.axis_index(axis), sizes[axis]
        from_ref = outs[source[1]] if isinstance(source, tuple) else ins[source]
        into_ref = outs[at]
        send, recv, own = sems[3 * at : 3 * at + 3]

        def part(peer):
            if kind == "gather":
                return from_ref
            if kind == "swap":
                return from_ref.at[peer]
            run = from_ref.shape[0] // count
            return from_ref.at[pl.ds(peer * run, run)]

        if not with_remote:
            return [pltpu.make_async_copy(part(me), into_ref.at[me], own)]
        found = []
        for step in range(1, count):
            peer = lax.rem(me + step, count)
            found.append(
                pltpu.make_async_remote_copy(
                    src_ref=part(peer),
                    dst_ref=into_ref.at[me],
                    send_sem=send.at[step - 1],
                    recv_sem=recv.at[step - 1],
                    device_id={axis: peer},
                    device_id_type=MESH,
                )
            )
        return found

    first = [at for at in range(len(jobs)) if not isinstance(jobs[at][2], tuple)]
    later = [at for at in range(len(jobs)) if isinstance(jobs[at][2], tuple)]
    flying = {at: local_and_remote(at, False) for at in first}
    for at in first:
        for copy in flying[at]:
            copy.start()
    pl.semaphore_wait(barrier, total)
    first.sort(key=lambda at: not any(jobs[other][2] == ("out", at) for other in later))
    for at in first:
        more = local_and_remote(at, True)
        for copy in more:
            copy.start()
        flying[at] += more
    for at in later:
        for copy in flying.pop(jobs[at][2][1]):
            copy.wait()
        flying[at] = local_and_remote(at, False) + local_and_remote(at, True)
        for copy in flying[at]:
            copy.start()
    for copies in flying.values():
        for copy in copies:
            copy.wait()


def exchange(mark, jobs, *arrays):
    sizes = {"dp": lax.axis_size("dp"), "rep": lax.axis_size("rep")}
    shapes = []
    for axis, kind, source in jobs:
        like = shapes[source[1]] if isinstance(source, tuple) else arrays[source]
        count = sizes[axis]
        if kind == "gather":
            shape = (count,) + tuple(like.shape)
        elif kind == "swap":
            shape = tuple(like.shape)
        else:
            shape = (count, like.shape[0] // count) + tuple(like.shape[1:])
        shapes.append(jax.ShapeDtypeStruct(shape, like.dtype))
    scratch = []
    for axis, _, _ in jobs:
        scratch += [
            pltpu.SemaphoreType.DMA((sizes[axis] - 1,)),
            pltpu.SemaphoreType.DMA((sizes[axis] - 1,)),
            pltpu.SemaphoreType.DMA,
        ]
    return pl.pallas_call(
        functools.partial(exchange_kernel, jobs, sizes, len(arrays)),
        out_shape=tuple(shapes),
        in_specs=[pl.BlockSpec(memory_space=pl.ANY)] * len(arrays),
        out_specs=tuple([pl.BlockSpec(memory_space=pl.ANY)] * len(jobs)),
        scratch_shapes=scratch,
        compiler_params=pltpu.CompilerParams(collective_id=mark, has_side_effects=True),
        name="exchange_%d" % mark,
    )(*arrays)


def attend_kernel(heads, block, qkv_ref, line_ref, seg_col_ref, seg_row_ref, probs_ref, mix_ref):
    rows = qkv_ref.shape[0]
    width = heads * HEAD
    for head in range(heads):
        low = head * HEAD
        k_head = qkv_ref[:, width + low : width + low + HEAD]
        v_head = qkv_ref[:, 2 * width + low : 2 * width + low + HEAD]
        line = line_ref[head : head + 1, :]
        span = line.shape[1]
        for start in range(0, rows, block):
            q_part = qkv_ref[start : start + block, low : low + HEAD]
            bias = pltpu.roll(
                jnp.broadcast_to(line, (block, span)), start, 1, stride=1, stride_axis=0
            )[:, :rows]
            scores = dot_over(q_part, k_head, 1, 1) * HEAD ** (-0.5) + bias
            allowed = seg_col_ref[start : start + block, :] == seg_row_ref[...]
            scores = jnp.where(allowed, scores, NEG)
            raised = jnp.exp(scores - jnp.max(scores, axis=-1, keepdims=True))
            probs = raised * (1.0 / jnp.sum(raised, axis=-1, keepdims=True))
            probs_ref[head, start : start + block, :] = probs
            mix_ref[start : start + block, low : low + HEAD] = matmul(
                probs.astype(jnp.bfloat16), v_head
            ).astype(jnp.bfloat16)


def attend(qkv, line, seg_col, seg_row, heads, block):
    rows = qkv.shape[0]
    return pl.pallas_call(
        functools.partial(attend_kernel, heads, block),
        out_shape=(
            jax.ShapeDtypeStruct((heads, rows, rows), jnp.float32),
            jax.ShapeDtypeStruct((rows, heads * HEAD), jnp.bfloat16),
        ),
        compiler_params=pltpu.CompilerParams(vmem_limit_bytes=VMEM_LIMIT),
        name="attend",
    )(qkv, line, seg_col, seg_row)


def attend_back_kernel(heads, block, qkv_ref, dmix_ref, probs_ref, dqkv_ref, dline_ref):
    rows = qkv_ref.shape[0]
    width = heads * HEAD
    span = dline_ref.shape[1]
    scale = HEAD ** (-0.5)
    for head in range(heads):
        low = head * HEAD
        k_head = qkv_ref[:, width + low : width + low + HEAD]
        v_head = qkv_ref[:, 2 * width + low : 2 * width + low + HEAD]
        dk = jnp.zeros((rows, HEAD), jnp.float32)
        dv = jnp.zeros((rows, HEAD), jnp.float32)
        dline = jnp.zeros((1, span), jnp.float32)
        for start in range(0, rows, block):
            q_part = qkv_ref[start : start + block, low : low + HEAD]
            dmix = dmix_ref[start : start + block, low : low + HEAD]
            probs = probs_ref[head, start : start + block, :]
            dprobs = dot_over(dmix, v_head, 1, 1)
            dscores = probs * (dprobs - jnp.sum(probs * dprobs, axis=-1, keepdims=True))
            low_scores = dscores.astype(jnp.bfloat16)
            dqkv_ref[start : start + block, low : low + HEAD] = (
                matmul(low_scores, k_head) * scale
            ).astype(jnp.bfloat16)
            dk = dk + dot_over(low_scores, q_part, 0, 0)
            dv = dv + dot_over(probs.astype(jnp.bfloat16), dmix, 0, 0)
            fold = jnp.concatenate(
                [dscores, jnp.zeros((block, span - rows), jnp.float32)], axis=1
            )
            half = block // 2
            while half >= 1:
                fold = fold[:half] + pltpu.roll(fold[half:], span - half, 1)
                half //= 2
            dline = dline + (pltpu.roll(fold, span - start, 1) if start else fold)
        dqkv_ref[:, width + low : width + low + HEAD] = (dk * scale).astype(jnp.bfloat16)
        dqkv_ref[:, 2 * width + low : 2 * width + low + HEAD] = dv.astype(jnp.bfloat16)
        dline_ref[head : head + 1, :] = dline


def attend_back(qkv, dmix, probs, heads, block):
    rows = qkv.shape[0]
    return pl.pallas_call(
        functools.partial(attend_back_kernel, heads, block),
        out_shape=(
            jax.ShapeDtypeStruct(qkv.shape, jnp.bfloat16),
            jax.ShapeDtypeStruct((heads, 2 * rows), jnp.float32),
        ),
        compiler_params=pltpu.CompilerParams(vmem_limit_bytes=VMEM_LIMIT),
        name="attend_back",
    )(qkv, dmix, probs)


def closing_kernel(
    sizes,
    tile,
    grads_ref,
    small_ref,
    got_ref,
    w_in_ref,
    w_out_ref,
    weight_all_ref,
    small_all_ref,
    dw_in_ref,
    dw_out_ref,
    got_here,
    w_in_here,
    w_out_here,
    dw_in_here,
    dw_out_here,
    land,
    small_land,
    piece,
    small_piece,
    load_sems,
    store_sems,
    own_sems,
    dp_send,
    dp_recv,
    rep_send,
    rep_recv,
):
    places = {axis: lax.axis_index(axis) for axis in ("dp", "rep")}
    barrier = pltpu.get_barrier_semaphore()
    for axis in ("dp", "rep"):
        for step in range(1, sizes[axis]):
            peer = lax.rem(places[axis] + step, sizes[axis])
            pl.semaphore_signal(barrier, inc=1, device_id={axis: peer}, device_id_type=MESH)
    dp_at, rep_at = places["dp"], places["rep"]
    own = [
        pltpu.make_async_copy(grads_ref.at[dp_at], land.at[dp_at], own_sems.at[0]),
        pltpu.make_async_copy(small_ref.at[dp_at], small_land.at[dp_at], own_sems.at[1]),
    ]
    loads = [
        pltpu.make_async_copy(got_ref, got_here, load_sems.at[0]),
        pltpu.make_async_copy(w_in_ref, w_in_here, load_sems.at[1]),
        pltpu.make_async_copy(w_out_ref, w_out_here, load_sems.at[2]),
    ]
    for copy in own + loads:
        copy.start()
    pl.semaphore_wait(barrier, sizes["dp"] + sizes["rep"] - 2)
    across = []
    for step in range(1, sizes["dp"]):
        peer = lax.rem(dp_at + step, sizes["dp"])
        for at, (from_ref, into_ref) in enumerate(((grads_ref, land), (small_ref, small_land))):
            across.append(
                pltpu.make_async_remote_copy(
                    src_ref=from_ref.at[peer],
                    dst_ref=into_ref.at[dp_at],
                    send_sem=dp_send.at[at, step - 1],
                    recv_sem=dp_recv.at[at, step - 1],
                    device_id={"dp": peer},
                    device_id_type=MESH,
                )
            )
    for copy in across:
        copy.start()
    for copy in loads:
        copy.wait()

    model_width = w_in_ref.shape[0]
    tiles = w_in_ref.shape[1] // tile

    def stores(at):
        here = pl.ds(pl.multiple_of(at * tile, tile), tile)
        return (
            pltpu.make_async_copy(
                dw_in_here.at[:, here], dw_in_ref.at[:, here], store_sems.at[0, at]
            ),
            pltpu.make_async_copy(dw_out_here.at[here], dw_out_ref.at[here], store_sems.at[1, at]),
        )

    def one_tile(at, carry):
        here = pl.ds(pl.multiple_of(at * tile, tile), tile)
        rows, grads = got_here[:, :model_width], got_here[:, model_width:]
        pre = matmul(rows, w_in_here[:, here])
        squared = pre * pre
        bent = jnp.tanh(0.7978845608028654 * pre * (1.0 + 0.044715 * squared))
        half = 0.5 * (1.0 + bent)
        slope = half + 0.5 * pre * (1.0 - bent * bent) * (
            0.7978845608028654 * (1.0 + 3.0 * 0.044715 * squared)
        )
        act = (pre * half).astype(jnp.bfloat16)
        dpre = (dot_over(grads, w_out_here[here, :], 1, 1) * slope).astype(jnp.bfloat16)
        dw_in_here[:, here] = dot_over(rows, dpre, 0, 0).astype(jnp.bfloat16)
        dw_out_here[here, :] = dot_over(act, grads, 0, 0).astype(jnp.bfloat16)
        for copy in stores(at):
            copy.start()
        return carry

    early = tiles - tiles // 4
    lax.fori_loop(0, early, one_tile, 0)
    for copy in own + across:
        copy.wait()
    total = land[0].astype(jnp.float32)
    small_total = small_land[0]
    for at in range(1, sizes["dp"]):
        total = total + land[at].astype(jnp.float32)
        small_total = small_total + small_land[at]
    piece[...] = total.astype(jnp.bfloat16)
    small_piece[...] = small_total
    last = [
        pltpu.make_async_copy(piece, weight_all_ref.at[rep_at], own_sems.at[2]),
        pltpu.make_async_copy(small_piece, small_all_ref.at[rep_at], own_sems.at[3]),
    ]
    for step in range(1, sizes["rep"]):
        peer = lax.rem(rep_at + step, sizes["rep"])
        for at, (from_ref, into_ref) in enumerate(
            ((piece, weight_all_ref), (small_piece, small_all_ref))
        ):
            last.append(
                pltpu.make_async_remote_copy(
                    src_ref=from_ref,
                    dst_ref=into_ref.at[rep_at],
                    send_sem=rep_send.at[at, step - 1],
                    recv_sem=rep_recv.at[at, step - 1],
                    device_id={"rep": peer},
                    device_id_type=MESH,
                )
            )
    for copy in last:
        copy.start()
    lax.fori_loop(early, tiles, one_tile, 0)

    def finish(at, carry):
        for copy in stores(at):
            copy.wait()
        return carry

    lax.fori_loop(0, tiles, finish, 0)
    for copy in last:
        copy.wait()


def closing(mark, grads, small, got, w_in, w_out):
    sizes = {"dp": lax.axis_size("dp"), "rep": lax.axis_size("rep")}
    hidden = w_in.shape[1]
    tile = 256 if hidden % 256 == 0 else 128
    rest = pl.BlockSpec(memory_space=pl.ANY)
    low_type = jnp.bfloat16
    dma = pltpu.SemaphoreType.DMA
    return pl.pallas_call(
        functools.partial(closing_kernel, sizes, tile),
        out_shape=(
            jax.ShapeDtypeStruct((sizes["rep"],) + grads.shape[1:], low_type),
            jax.ShapeDtypeStruct((sizes["rep"],) + small.shape[1:], jnp.float32),
            jax.ShapeDtypeStruct(w_in.shape, low_type),
            jax.ShapeDtypeStruct(w_out.shape, low_type),
        ),
        in_specs=[rest] * 5,
        out_specs=(rest,) * 4,
        scratch_shapes=[
            pltpu.VMEM(got.shape, low_type),
            pltpu.VMEM(w_in.shape, low_type),
            pltpu.VMEM(w_out.shape, low_type),
            pltpu.VMEM(w_in.shape, low_type),
            pltpu.VMEM(w_out.shape, low_type),
            pltpu.VMEM(grads.shape, low_type),
            pltpu.VMEM(small.shape, jnp.float32),
            pltpu.VMEM(grads.shape[1:], low_type),
            pltpu.VMEM(small.shape[1:], jnp.float32),
            dma((3,)),
            dma((2, hidden // tile)),
            dma((4,)),
            dma((2, sizes["dp"] - 1)),
            dma((2, sizes["dp"] - 1)),
            dma((2, sizes["rep"] - 1)),
            dma((2, sizes["rep"] - 1)),
        ],
        compiler_params=pltpu.CompilerParams(
            collective_id=mark, has_side_effects=True, vmem_limit_bytes=VMEM_LIMIT
        ),
        name="closing",
    )(grads, small, got, w_in, w_out)


def packed(parts, lead):
    flat = jnp.concatenate([piece.reshape(lead + (-1,)) for piece in parts], axis=-1)
    count = flat.shape[-1]
    whole = -(-count // 1024) * 1024
    flat = jnp.pad(flat, [(0, 0)] * len(lead) + [(0, whole - count)])
    return flat.reshape(lead + (whole // 128, 128))


def unpacked(flat, widths):
    found, at = [], 0
    for width in widths:
        found.append(flat[..., at : at + width])
        at += width
    return found


def local_columns(full, width, place):
    return lax.dynamic_slice_in_dim(full, place * width, width, axis=1)


def on_device(
    tokens,
    seq_lengths,
    bucket_ids,
    routes,
    norm1_gain,
    w_query,
    w_key,
    w_value,
    w_output,
    rel_bias,
    norm2_gain,
    w_router,
    w_in,
    w_out,
    cotangent,
):
    row_count, model_width = tokens.shape
    dp_count, rep_count = lax.axis_size("dp"), lax.axis_size("rep")
    rep_at = lax.axis_index("rep")
    group_rows = row_count * rep_count
    first_row = rep_at * row_count
    split_count = dp_count // EXPERTS
    capacity = row_count // 8 + row_count // 64
    heads = HEADS // rep_count
    width = heads * HEAD
    shard = w_query.shape[0]
    low_type = jnp.bfloat16

    piece_qkv = jnp.concatenate(
        [local_columns(full, width, rep_at) for full in (w_query, w_key, w_value)], axis=1
    )
    piece_out = local_columns(w_output, width, rep_at)
    small_widths = (shard, shard, rel_bias.shape[0], shard * EXPERTS)
    small = packed(
        [x.astype(jnp.float32) for x in (norm1_gain, norm2_gain, rel_bias, w_router)], ()
    )
    qkv_parts, out_parts, small_parts, token_parts, out_rows = exchange(
        1,
        (
            ("dp", "gather", 0),
            ("dp", "gather", 1),
            ("dp", "gather", 2),
            ("rep", "gather", 3),
            ("rep", "blocks", ("out", 1)),
        ),
        piece_qkv,
        piece_out,
        small,
        tokens,
    )
    w_qkv = qkv_parts.reshape(model_width, 3 * width)
    w_out_rows = (
        out_rows.reshape(rep_count, width, width).transpose(1, 0, 2).reshape(width, model_width)
    )
    gain_one, gain_two, table_flat, router_flat = unpacked(
        small_parts.reshape(dp_count, -1), small_widths
    )
    gain_first = gain_one.reshape(model_width)
    gain_second = gain_two.reshape(model_width)
    router_full = router_flat.reshape(model_width, EXPERTS).astype(low_type)
    table = lax.dynamic_slice_in_dim(table_flat.reshape(HEADS, BUCKETS), rep_at * heads, heads, 0)

    seq_ends = jnp.cumsum(seq_lengths[0])
    places = jnp.arange(group_rows, dtype=jnp.int32)
    segment = jnp.sum((places[:, None] >= seq_ends[None, :]).astype(jnp.int32), axis=1)
    live_bool = first_row + jnp.arange(row_count, dtype=jnp.int32) < seq_ends[-1]
    row_live = live_bool.astype(jnp.float32)[:, None]
    x_in = tokens.astype(jnp.float32)
    x_group = token_parts.reshape(group_rows, model_width).astype(jnp.float32)
    h_one = rms_scale(x_group, gain_first).astype(low_type)
    qkv = matmul(h_one, w_qkv).astype(low_type)

    by_step = jnp.concatenate(
        [
            bucket_ids[group_rows - 1 :: -1],
            jnp.full((1,), -1, jnp.int32),
            bucket_ids[: group_rows - 1 : -1],
        ]
    )
    bucket_hot = (by_step[None, :] == jnp.arange(BUCKETS, dtype=jnp.int32)[:, None]).astype(
        jnp.float32
    )
    line = jnp.dot(table, bucket_hot, precision=HIGH)
    probs, mixture = attend(qkv, line, segment[:, None], segment[None, :], heads, row_count)

    branch_parts = matmul(mixture, w_out_rows).astype(low_type)
    (branch_got,) = exchange(
        2,
        (("rep", "swap", 0),),
        branch_parts.reshape(rep_count, row_count, model_width),
    )
    branch = jnp.sum(branch_got.astype(jnp.float32), axis=0)
    x_one = x_in + row_live * branch
    h_two = rms_scale(x_one, gain_second).astype(low_type)
    router_probs = jax.nn.softmax(matmul(h_two, router_full), axis=-1)
    route_ids = routes[:, 0]
    route_onehot = route_ids[:, None] == jnp.arange(EXPERTS, dtype=jnp.int32)[None, :]
    gate_vals = jnp.sum(router_probs * route_onehot.astype(jnp.float32), axis=1, keepdims=True)
    chosen = route_onehot & live_bool[:, None]
    before = (
        jnp.arange(row_count, dtype=jnp.int32)[:, None]
        >= jnp.arange(row_count, dtype=jnp.int32)[None, :]
    ).astype(low_type)
    counts = matmul(before, chosen.astype(low_type)).astype(jnp.int32)
    rank_in = jnp.sum(jnp.where(chosen, counts - 1, 0), axis=1)
    slot_ids = jnp.where(live_bool, route_ids * capacity + rank_in, -1)
    slot_of = jnp.arange(dp_count * capacity, dtype=jnp.int32)
    slot_of = (slot_of // (capacity * split_count)) * capacity + slot_of % capacity
    dispatch = (slot_of[:, None] == slot_ids[None, :]).astype(low_type)

    grad_out = cotangent.astype(jnp.float32)
    grad_expert = (gate_vals * row_live * grad_out).astype(low_type)
    sent = matmul(dispatch, jnp.concatenate([h_two, grad_expert], axis=1)).astype(low_type)
    (got,) = exchange(
        3, (("dp", "swap", 0),), sent.reshape(dp_count, capacity, 2 * model_width)
    )
    got = got.reshape(dp_count * capacity, 2 * model_width)
    rows_here, grads_here = got[:, :model_width], got[:, model_width:]

    def expert(rows, grads):
        pre = matmul(rows, w_in)
        act, pull = jax.vjp(lambda inner: jax.nn.gelu(inner, approximate=True), pre)
        dpre = pull(dot_over(grads, w_out, 1, 1))[0]
        return act.astype(low_type), dpre.astype(low_type)

    act_here, dpre_here = expert(rows_here, grads_here)
    back = jnp.concatenate(
        [matmul(act_here, w_out).astype(low_type), dot_over(dpre_here, w_in, 1, 1).astype(low_type)],
        axis=1,
    )
    returned, got_all = exchange(
        4,
        (("dp", "swap", 0), ("rep", "gather", 1)),
        back.reshape(dp_count, capacity, 2 * model_width),
        got,
    )
    landed = dot_over(dispatch, returned.reshape(dp_count * capacity, 2 * model_width), 0, 0)
    expert_rows, grad_h_two = landed[:, :model_width], landed[:, model_width:]

    block_out = x_one + gate_vals * expert_rows * row_live
    grad_gate = jnp.sum(grad_out * expert_rows, axis=1, keepdims=True) * row_live
    grad_probs = route_onehot.astype(jnp.float32) * grad_gate
    grad_logits = router_probs * (
        grad_probs - jnp.sum(router_probs * grad_probs, axis=1, keepdims=True)
    )
    grad_router = jnp.dot(h_two.astype(jnp.float32).T, grad_logits, precision=HIGH)
    grad_h_two = grad_h_two + jnp.dot(
        grad_logits, router_full.astype(jnp.float32).T, precision=HIGH
    )
    _, norm_two_pull = jax.vjp(rms_scale, x_one, gain_second)
    grad_x_norm, grad_gain_two = norm_two_pull(grad_h_two)
    grad_x_one = grad_out + grad_x_norm
    grad_branch = (grad_x_one * row_live).astype(low_type)

    (branch_all,) = exchange(5, (("rep", "gather", 0),), grad_branch)
    grad_branch_group = branch_all.reshape(group_rows, model_width)
    grad_w_output = dot_over(mixture, grad_branch_group, 0, 0).astype(low_type)
    dmix = dot_over(grad_branch_group, w_out_rows, 1, 1).astype(low_type)
    dqkv, dline = attend_back(qkv, dmix, probs, heads, row_count)
    grad_table = jnp.dot(dline, bucket_hot.T, precision=HIGH)
    grad_w_qkv = dot_over(h_one, dqkv, 0, 0).astype(low_type)
    grad_h_parts = dot_over(dqkv, w_qkv, 1, 1).astype(low_type)
    grad_h_got, grad_out_cols = exchange(
        6,
        (("rep", "swap", 0), ("rep", "swap", 1)),
        grad_h_parts.reshape(rep_count, row_count, model_width),
        grad_w_output.reshape(width, rep_count, width).transpose(1, 0, 2),
    )
    grad_h_one = jnp.sum(grad_h_got.astype(jnp.float32), axis=0)
    _, norm_one_pull = jax.vjp(rms_scale, x_in, gain_first)
    grad_x_in, grad_gain_one = norm_one_pull(grad_h_one)
    grad_input = grad_x_one + grad_x_in

    table_whole = lax.dynamic_update_slice_in_dim(
        jnp.zeros((HEADS, BUCKETS), jnp.float32), grad_table, rep_at * heads, 0
    )
    small_grads = packed(
        [
            x.reshape(dp_count, -1)
            for x in (grad_gain_one, grad_gain_two, table_whole, grad_router)
        ],
        (dp_count,),
    )
    weight_all, small_all, grad_w_in, grad_w_out = closing(
        7,
        jnp.concatenate(
            [
                grad_w_qkv.reshape(dp_count, shard, 3 * width),
                grad_out_cols.reshape(dp_count, shard, width),
            ],
            axis=2,
        ),
        small_grads,
        got_all.reshape(-1, 2 * model_width),
        w_in,
        w_out,
    )
    weights = (
        weight_all.reshape(rep_count, shard, 4, width)
        .transpose(2, 1, 0, 3)
        .reshape(4, shard, model_width)
        .astype(jnp.float32)
    )
    small_sum = jnp.sum(small_all, axis=0).reshape(-1)
    out_gain_one, out_gain_two, out_table, out_router = unpacked(small_sum, small_widths)

    return (
        block_out.astype(low_type),
        grad_input,
        out_gain_one,
        weights[0],
        weights[1],
        weights[2],
        weights[3],
        out_table,
        out_gain_two,
        out_router.reshape(shard, EXPERTS),
        grad_w_in.astype(jnp.float32),
        grad_w_out.astype(jnp.float32),
    )


def solution(mesh):
    placed = (
        P(("dp", "rep"), None),
        P("dp", None),
        P(),
        P(("dp", "rep"), None),
        P("dp"),
        P("dp", None),
        P("dp", None),
        P("dp", None),
        P("dp", None),
        P("dp"),
        P("dp"),
        P("dp", None),
        P(None, "dp"),
        P("dp", None),
        P(("dp", "rep"), None),
    )
    return jax.shard_map(
        on_device,
        mesh=mesh,
        in_specs=placed,
        out_specs=(
            P(("dp", "rep"), None),
            P(("dp", "rep"), None),
            P("dp"),
            P("dp", None),
            P("dp", None),
            P("dp", None),
            P("dp", None),
            P("dp"),
            P("dp"),
            P("dp", None),
            P(None, "dp"),
            P("dp", None),
        ),
        check_vma=False,
    )
```

```python
import functools

import jax
import jax.numpy as jnp
from jax import lax
from jax.experimental import pallas as pl
from jax.experimental.pallas import tpu as pltpu
from jax.sharding import PartitionSpec as P

HEADS = 12
HEAD = 64
BUCKETS = 32
EXPERTS = 8


EPS = 1e-06
NEG = -1e30
HIGH = lax.Precision.HIGHEST
MESH = pl.DeviceIdType.MESH
VMEM_LIMIT = 48 * 1024 * 1024


def rms_scale(rows_in, gain_vec):
    return rows_in * lax.rsqrt(jnp.mean(rows_in * rows_in, axis=-1, keepdims=True) + EPS) * gain_vec


def matmul(left_op, right_op):
    return jnp.dot(left_op, right_op, preferred_element_type=jnp.float32)


def dot_over(left_op, right_op, left_dim, right_dim):
    return lax.dot_general(
        left_op, right_op, (((left_dim,), (right_dim,)), ((), ())), preferred_element_type=jnp.float32
    )


def exchange_kernel(jobs, sizes, in_count, *refs):
    ins, outs = refs[:in_count], refs[in_count : in_count + len(jobs)]
    sems = refs[in_count + len(jobs) :]
    axes = []
    for axis, _, _ in jobs:
        if axis not in axes:
            axes.append(axis)
    barrier = pltpu.get_barrier_semaphore()
    total = 0
    for axis in axes:
        me, count = lax.axis_index(axis), sizes[axis]
        for step in range(1, count):
            peer = lax.rem(me + step, count)
            pl.semaphore_signal(barrier, inc=1, device_id={axis: peer}, device_id_type=MESH)
        total += count - 1

    def local_and_remote(at, with_remote):
        axis, kind, source = jobs[at]
        me, count = lax.axis_index(axis), sizes[axis]
        from_ref = outs[source[1]] if isinstance(source, tuple) else ins[source]
        into_ref = outs[at]
        send, recv, own = sems[3 * at : 3 * at + 3]

        def part(peer):
            if kind in ("gather", "relay"):
                return from_ref
            if kind == "swap":
                return from_ref.at[peer]
            run = from_ref.shape[0] // count
            return from_ref.at[pl.ds(peer * run, run)]

        if not with_remote:
            return [pltpu.make_async_copy(part(me), into_ref.at[me], own)]
        if kind == "relay":
            across, beside = lax.rem(me + 2, count), me + 1 - 2 * lax.rem(me, 2)
            hops = (
                (from_ref, me, across),
                (from_ref, me, beside),
                (into_ref.at[across], across, beside),
            )
            return [
                pltpu.make_async_remote_copy(
                    src_ref=source_ref,
                    dst_ref=into_ref.at[slot],
                    send_sem=send.at[hop],
                    recv_sem=recv.at[hop],
                    device_id={axis: peer},
                    device_id_type=MESH,
                )
                for hop, (source_ref, slot, peer) in enumerate(hops)
            ]
        found = []
        for step in range(1, count):
            peer = lax.rem(me + step, count)
            found.append(
                pltpu.make_async_remote_copy(
                    src_ref=part(peer),
                    dst_ref=into_ref.at[me],
                    send_sem=send.at[step - 1],
                    recv_sem=recv.at[step - 1],
                    device_id={axis: peer},
                    device_id_type=MESH,
                )
            )
        return found

    first = [at for at in range(len(jobs)) if not isinstance(jobs[at][2], tuple)]
    later = [at for at in range(len(jobs)) if isinstance(jobs[at][2], tuple)]
    flying = {at: local_and_remote(at, False) for at in first}
    for at in first:
        for copy in flying[at]:
            copy.start()
    pl.semaphore_wait(barrier, total)
    first.sort(key=lambda at: not any(jobs[other][2] == ("out", at) for other in later))
    for at in first:
        more = local_and_remote(at, True)
        for copy in more[: 2 if jobs[at][1] == "relay" else None]:
            copy.start()
        flying[at] += more
    for at in first:
        if jobs[at][1] == "relay":
            flying[at][1].wait()
            flying[at][3].start()
            del flying[at][1]
    for at in later:
        for copy in flying.pop(jobs[at][2][1]):
            copy.wait()
        flying[at] = local_and_remote(at, False) + local_and_remote(at, True)
        for copy in flying[at]:
            copy.start()
    for copies in flying.values():
        for copy in copies:
            copy.wait()


def exchange(mark, jobs, *arrays):
    sizes = {"dp": lax.axis_size("dp"), "rep": lax.axis_size("rep")}
    shapes = []
    for axis, kind, source in jobs:
        like = shapes[source[1]] if isinstance(source, tuple) else arrays[source]
        count = sizes[axis]
        if kind in ("gather", "relay"):
            shape = (count,) + tuple(like.shape)
        elif kind == "swap":
            shape = tuple(like.shape)
        else:
            shape = (count, like.shape[0] // count) + tuple(like.shape[1:])
        shapes.append(jax.ShapeDtypeStruct(shape, like.dtype))
    scratch = []
    for axis, _, _ in jobs:
        scratch += [
            pltpu.SemaphoreType.DMA((sizes[axis] - 1,)),
            pltpu.SemaphoreType.DMA((sizes[axis] - 1,)),
            pltpu.SemaphoreType.DMA,
        ]
    return pl.pallas_call(
        functools.partial(exchange_kernel, jobs, sizes, len(arrays)),
        out_shape=tuple(shapes),
        in_specs=[pl.BlockSpec(memory_space=pl.ANY)] * len(arrays),
        out_specs=tuple([pl.BlockSpec(memory_space=pl.ANY)] * len(jobs)),
        scratch_shapes=scratch,
        compiler_params=pltpu.CompilerParams(collective_id=mark, has_side_effects=True),
        name="exchange_%d" % mark,
    )(*arrays)


def attend_kernel(heads, block, qkv_ref, line_ref, seg_col_ref, seg_row_ref, probs_ref, mix_ref):
    rows = qkv_ref.shape[0]
    width = heads * HEAD
    for head in range(heads):
        low = head * HEAD
        k_head = qkv_ref[:, width + low : width + low + HEAD]
        v_head = qkv_ref[:, 2 * width + low : 2 * width + low + HEAD]
        line = line_ref[head : head + 1, :]
        span = line.shape[1]
        for start in range(0, rows, block):
            q_part = qkv_ref[start : start + block, low : low + HEAD]
            bias = pltpu.roll(
                jnp.broadcast_to(line, (block, span)), start, 1, stride=1, stride_axis=0
            )[:, :rows]
            scores = dot_over(q_part, k_head, 1, 1) * HEAD ** (-0.5) + bias
            allowed = seg_col_ref[start : start + block, :] == seg_row_ref[...]
            scores = jnp.where(allowed, scores, NEG)
            raised = jnp.exp(scores - jnp.max(scores, axis=-1, keepdims=True))
            probs = raised * (1.0 / jnp.sum(raised, axis=-1, keepdims=True))
            probs_ref[head, start : start + block, :] = probs
            mix_ref[start : start + block, low : low + HEAD] = matmul(
                probs.astype(jnp.bfloat16), v_head
            ).astype(jnp.bfloat16)


def attend(qkv, line, seg_col, seg_row, heads, block):
    rows = qkv.shape[0]
    return pl.pallas_call(
        functools.partial(attend_kernel, heads, block),
        out_shape=(
            jax.ShapeDtypeStruct((heads, rows, rows), jnp.float32),
            jax.ShapeDtypeStruct((rows, heads * HEAD), jnp.bfloat16),
        ),
        compiler_params=pltpu.CompilerParams(vmem_limit_bytes=VMEM_LIMIT),
        name="attend",
    )(qkv, line, seg_col, seg_row)


def attend_back_kernel(heads, block, qkv_ref, dmix_ref, probs_ref, dqkv_ref, dline_ref):
    rows = qkv_ref.shape[0]
    width = heads * HEAD
    span = dline_ref.shape[1]
    scale = HEAD ** (-0.5)
    for head in range(heads):
        low = head * HEAD
        k_head = qkv_ref[:, width + low : width + low + HEAD]
        v_head = qkv_ref[:, 2 * width + low : 2 * width + low + HEAD]
        dk = jnp.zeros((rows, HEAD), jnp.float32)
        dv = jnp.zeros((rows, HEAD), jnp.float32)
        dline = jnp.zeros((1, span), jnp.float32)
        for start in range(0, rows, block):
            q_part = qkv_ref[start : start + block, low : low + HEAD]
            dmix = dmix_ref[start : start + block, low : low + HEAD]
            probs = probs_ref[head, start : start + block, :]
            dprobs = dot_over(dmix, v_head, 1, 1)
            dscores = probs * (dprobs - jnp.sum(probs * dprobs, axis=-1, keepdims=True))
            low_scores = dscores.astype(jnp.bfloat16)
            dqkv_ref[start : start + block, low : low + HEAD] = (
                matmul(low_scores, k_head) * scale
            ).astype(jnp.bfloat16)
            dk = dk + dot_over(low_scores, q_part, 0, 0)
            dv = dv + dot_over(probs.astype(jnp.bfloat16), dmix, 0, 0)
            fold = jnp.concatenate(
                [dscores, jnp.zeros((block, span - rows), jnp.float32)], axis=1
            )
            half = block // 2
            while half >= 1:
                fold = fold[:half] + pltpu.roll(fold[half:], span - half, 1)
                half //= 2
            dline = dline + (pltpu.roll(fold, span - start, 1) if start else fold)
        dqkv_ref[:, width + low : width + low + HEAD] = (dk * scale).astype(jnp.bfloat16)
        dqkv_ref[:, 2 * width + low : 2 * width + low + HEAD] = dv.astype(jnp.bfloat16)
        dline_ref[head : head + 1, :] = dline


def attend_back(qkv, dmix, probs, heads, block):
    rows = qkv.shape[0]
    return pl.pallas_call(
        functools.partial(attend_back_kernel, heads, block),
        out_shape=(
            jax.ShapeDtypeStruct(qkv.shape, jnp.bfloat16),
            jax.ShapeDtypeStruct((heads, 2 * rows), jnp.float32),
        ),
        compiler_params=pltpu.CompilerParams(vmem_limit_bytes=VMEM_LIMIT),
        name="attend_back",
    )(qkv, dmix, probs)


def gelu_and_slope(pre):
    squared = pre * pre
    bent = jnp.tanh(0.7978845608028654 * pre * (1.0 + 0.044715 * squared))
    half = 0.5 * (1.0 + bent)
    slope = half + 0.5 * pre * (1.0 - bent * bent) * (
        0.7978845608028654 * (1.0 + 3.0 * 0.044715 * squared)
    )
    return pre * half, slope


def expert_kernel(got_ref, w_in_ref, w_out_ref, back_ref, total):
    step = pl.program_id(0)
    model_width = w_in_ref.shape[0]
    rows, grads = got_ref[:, :model_width], got_ref[:, model_width:]
    act, slope = gelu_and_slope(matmul(rows, w_in_ref[...]))
    dpre = (dot_over(grads, w_out_ref[...], 1, 1) * slope).astype(jnp.bfloat16)

    @pl.when(step == 0)
    def _():
        total[...] = jnp.zeros_like(total)

    total[:, :model_width] += matmul(act.astype(jnp.bfloat16), w_out_ref[...])
    total[:, model_width:] += dot_over(dpre, w_in_ref[...], 1, 1)

    @pl.when(step == pl.num_programs(0) - 1)
    def _():
        back_ref[...] = total[...].astype(jnp.bfloat16)


def expert_rows_both_ways(got, w_in, w_out):
    model_width, hidden = w_in.shape
    tile = 512 if hidden % 512 == 0 else 128
    whole = pl.BlockSpec(got.shape, lambda step: (0, 0))
    return pl.pallas_call(
        expert_kernel,
        grid=(hidden // tile,),
        out_shape=jax.ShapeDtypeStruct(got.shape, jnp.bfloat16),
        in_specs=[
            whole,
            pl.BlockSpec((model_width, tile), lambda step: (0, step)),
            pl.BlockSpec((tile, model_width), lambda step: (step, 0)),
        ],
        out_specs=whole,
        scratch_shapes=[pltpu.VMEM(got.shape, jnp.float32)],
        compiler_params=pltpu.CompilerParams(vmem_limit_bytes=VMEM_LIMIT),
        name="expert_rows",
    )(got, w_in, w_out)


def closing_kernel(
    sizes,
    tile,
    grads_ref,
    small_ref,
    got_ref,
    w_in_ref,
    w_out_ref,
    weight_all_ref,
    small_all_ref,
    dw_in_ref,
    dw_out_ref,
    got_here,
    w_in_here,
    w_out_here,
    dw_in_here,
    dw_out_here,
    land,
    small_land,
    piece,
    small_piece,
    load_sems,
    store_sems,
    own_sems,
    dp_send,
    dp_recv,
    rep_send,
    rep_recv,
):
    places = {axis: lax.axis_index(axis) for axis in ("dp", "rep")}
    barrier = pltpu.get_barrier_semaphore()
    for axis in ("dp", "rep"):
        for step in range(1, sizes[axis]):
            peer = lax.rem(places[axis] + step, sizes[axis])
            pl.semaphore_signal(barrier, inc=1, device_id={axis: peer}, device_id_type=MESH)
    dp_at, rep_at = places["dp"], places["rep"]
    own = [
        pltpu.make_async_copy(grads_ref.at[dp_at], land.at[dp_at], own_sems.at[0]),
        pltpu.make_async_copy(small_ref.at[dp_at], small_land.at[dp_at], own_sems.at[1]),
    ]
    loads = [
        pltpu.make_async_copy(got_ref, got_here, load_sems.at[0]),
        pltpu.make_async_copy(w_in_ref, w_in_here, load_sems.at[1]),
        pltpu.make_async_copy(w_out_ref, w_out_here, load_sems.at[2]),
    ]
    for copy in own + loads:
        copy.start()
    pl.semaphore_wait(barrier, sizes["dp"] + sizes["rep"] - 2)
    across = []
    for step in range(1, sizes["dp"]):
        peer = lax.rem(dp_at + step, sizes["dp"])
        for at, (from_ref, into_ref) in enumerate(((grads_ref, land), (small_ref, small_land))):
            across.append(
                pltpu.make_async_remote_copy(
                    src_ref=from_ref.at[peer],
                    dst_ref=into_ref.at[dp_at],
                    send_sem=dp_send.at[at, step - 1],
                    recv_sem=dp_recv.at[at, step - 1],
                    device_id={"dp": peer},
                    device_id_type=MESH,
                )
            )
    for copy in across:
        copy.start()
    for copy in loads:
        copy.wait()

    model_width = w_in_ref.shape[0]
    tiles = w_in_ref.shape[1] // tile

    def stores(at):
        here = pl.ds(pl.multiple_of(at * tile, tile), tile)
        return (
            pltpu.make_async_copy(
                dw_in_here.at[:, here], dw_in_ref.at[:, here], store_sems.at[0, at]
            ),
            pltpu.make_async_copy(dw_out_here.at[here], dw_out_ref.at[here], store_sems.at[1, at]),
        )

    def one_tile(at, carry):
        here = pl.ds(pl.multiple_of(at * tile, tile), tile)
        rows, grads = got_here[:, :model_width], got_here[:, model_width:]
        pre = matmul(rows, w_in_here[:, here])
        act, slope = gelu_and_slope(pre)
        act = act.astype(jnp.bfloat16)
        dpre = (dot_over(grads, w_out_here[here, :], 1, 1) * slope).astype(jnp.bfloat16)
        dw_in_here[:, here] = dot_over(rows, dpre, 0, 0).astype(jnp.bfloat16)
        dw_out_here[here, :] = dot_over(act, grads, 0, 0).astype(jnp.bfloat16)
        for copy in stores(at):
            copy.start()
        return carry

    early = tiles - tiles // 4
    lax.fori_loop(0, early, one_tile, 0)
    for copy in own + across:
        copy.wait()
    total = land[0].astype(jnp.float32)
    small_total = small_land[0]
    for at in range(1, sizes["dp"]):
        total = total + land[at].astype(jnp.float32)
        small_total = small_total + small_land[at]
    piece[...] = total.astype(jnp.bfloat16)
    small_piece[...] = small_total
    last = [
        pltpu.make_async_copy(piece, weight_all_ref.at[rep_at], own_sems.at[2]),
        pltpu.make_async_copy(small_piece, small_all_ref.at[rep_at], own_sems.at[3]),
    ]
    for step in range(1, sizes["rep"]):
        peer = lax.rem(rep_at + step, sizes["rep"])
        for at, (from_ref, into_ref) in enumerate(
            ((piece, weight_all_ref), (small_piece, small_all_ref))
        ):
            last.append(
                pltpu.make_async_remote_copy(
                    src_ref=from_ref,
                    dst_ref=into_ref.at[rep_at],
                    send_sem=rep_send.at[at, step - 1],
                    recv_sem=rep_recv.at[at, step - 1],
                    device_id={"rep": peer},
                    device_id_type=MESH,
                )
            )
    for copy in last:
        copy.start()
    lax.fori_loop(early, tiles, one_tile, 0)

    def finish(at, carry):
        for copy in stores(at):
            copy.wait()
        return carry

    lax.fori_loop(0, tiles, finish, 0)
    for copy in last:
        copy.wait()


def closing(mark, grads, small, got, w_in, w_out):
    sizes = {"dp": lax.axis_size("dp"), "rep": lax.axis_size("rep")}
    hidden = w_in.shape[1]
    tile = 256 if hidden % 256 == 0 else 128
    rest = pl.BlockSpec(memory_space=pl.ANY)
    low_type = jnp.bfloat16
    dma = pltpu.SemaphoreType.DMA
    return pl.pallas_call(
        functools.partial(closing_kernel, sizes, tile),
        out_shape=(
            jax.ShapeDtypeStruct((sizes["rep"],) + grads.shape[1:], low_type),
            jax.ShapeDtypeStruct((sizes["rep"],) + small.shape[1:], jnp.float32),
            jax.ShapeDtypeStruct(w_in.shape, low_type),
            jax.ShapeDtypeStruct(w_out.shape, low_type),
        ),
        in_specs=[rest] * 5,
        out_specs=(rest,) * 4,
        scratch_shapes=[
            pltpu.VMEM(got.shape, low_type),
            pltpu.VMEM(w_in.shape, low_type),
            pltpu.VMEM(w_out.shape, low_type),
            pltpu.VMEM(w_in.shape, low_type),
            pltpu.VMEM(w_out.shape, low_type),
            pltpu.VMEM(grads.shape, low_type),
            pltpu.VMEM(small.shape, jnp.float32),
            pltpu.VMEM(grads.shape[1:], low_type),
            pltpu.VMEM(small.shape[1:], jnp.float32),
            dma((3,)),
            dma((2, hidden // tile)),
            dma((4,)),
            dma((2, sizes["dp"] - 1)),
            dma((2, sizes["dp"] - 1)),
            dma((2, sizes["rep"] - 1)),
            dma((2, sizes["rep"] - 1)),
        ],
        compiler_params=pltpu.CompilerParams(
            collective_id=mark, has_side_effects=True, vmem_limit_bytes=VMEM_LIMIT
        ),
        name="closing",
    )(grads, small, got, w_in, w_out)


def packed(parts, lead):
    flat = jnp.concatenate([piece.reshape(lead + (-1,)) for piece in parts], axis=-1)
    count = flat.shape[-1]
    whole = -(-count // 1024) * 1024
    flat = jnp.pad(flat, [(0, 0)] * len(lead) + [(0, whole - count)])
    return flat.reshape(lead + (whole // 128, 128))


def unpacked(flat, widths):
    found, at = [], 0
    for width in widths:
        found.append(flat[..., at : at + width])
        at += width
    return found


def local_columns(full, width, place):
    return lax.dynamic_slice_in_dim(full, place * width, width, axis=1)


def on_device(
    tokens,
    seq_lengths,
    bucket_ids,
    routes,
    norm1_gain,
    w_query,
    w_key,
    w_value,
    w_output,
    rel_bias,
    norm2_gain,
    w_router,
    w_in,
    w_out,
    cotangent,
):
    row_count, model_width = tokens.shape
    dp_count, rep_count = lax.axis_size("dp"), lax.axis_size("rep")
    rep_at = lax.axis_index("rep")
    group_rows = row_count * rep_count
    first_row = rep_at * row_count
    split_count = dp_count // EXPERTS
    capacity = row_count // 8 + row_count // 64
    heads = HEADS // rep_count
    width = heads * HEAD
    shard = w_query.shape[0]
    low_type = jnp.bfloat16
    spread_kind = "relay" if rep_count == 4 else "gather"

    piece_qkv = jnp.concatenate(
        [local_columns(full, width, rep_at) for full in (w_query, w_key, w_value)], axis=1
    )
    piece_out = local_columns(w_output, width, rep_at)
    small_widths = (shard, shard, rel_bias.shape[0], shard * EXPERTS)
    small = packed(
        [x.astype(jnp.float32) for x in (norm1_gain, norm2_gain, rel_bias, w_router)], ()
    )
    qkv_parts, out_parts, small_parts, token_parts, out_rows = exchange(
        1,
        (
            ("dp", "gather", 0),
            ("dp", "gather", 1),
            ("dp", "gather", 2),
            ("rep", "gather", 3),
            ("rep", "blocks", ("out", 1)),
        ),
        piece_qkv,
        piece_out,
        small,
        tokens,
    )
    w_qkv = qkv_parts.reshape(model_width, 3 * width)
    w_out_rows = (
        out_rows.reshape(rep_count, width, width).transpose(1, 0, 2).reshape(width, model_width)
    )
    gain_one, gain_two, table_flat, router_flat = unpacked(
        small_parts.reshape(dp_count, -1), small_widths
    )
    gain_first = gain_one.reshape(model_width)
    gain_second = gain_two.reshape(model_width)
    router_full = router_flat.reshape(model_width, EXPERTS).astype(low_type)
    table = lax.dynamic_slice_in_dim(table_flat.reshape(HEADS, BUCKETS), rep_at * heads, heads, 0)

    seq_ends = jnp.cumsum(seq_lengths[0])
    places = jnp.arange(group_rows, dtype=jnp.int32)
    segment = jnp.sum((places[:, None] >= seq_ends[None, :]).astype(jnp.int32), axis=1)
    live_bool = first_row + jnp.arange(row_count, dtype=jnp.int32) < seq_ends[-1]
    row_live = live_bool.astype(jnp.float32)[:, None]
    x_in = tokens.astype(jnp.float32)
    x_group = token_parts.reshape(group_rows, model_width).astype(jnp.float32)
    h_one = rms_scale(x_group, gain_first).astype(low_type)
    qkv = matmul(h_one, w_qkv).astype(low_type)

    by_step = jnp.concatenate(
        [
            bucket_ids[group_rows - 1 :: -1],
            jnp.full((1,), -1, jnp.int32),
            bucket_ids[: group_rows - 1 : -1],
        ]
    )
    bucket_hot = (by_step[None, :] == jnp.arange(BUCKETS, dtype=jnp.int32)[:, None]).astype(
        jnp.float32
    )
    line = jnp.dot(table, bucket_hot, precision=HIGH)
    probs, mixture = attend(qkv, line, segment[:, None], segment[None, :], heads, row_count)

    branch_parts = matmul(mixture, w_out_rows).astype(low_type)
    (branch_got,) = exchange(
        2,
        (("rep", "swap", 0),),
        branch_parts.reshape(rep_count, row_count, model_width),
    )
    branch = jnp.sum(branch_got.astype(jnp.float32), axis=0)
    x_one = x_in + row_live * branch
    h_two = rms_scale(x_one, gain_second).astype(low_type)
    router_probs = jax.nn.softmax(matmul(h_two, router_full), axis=-1)
    route_ids = routes[:, 0]
    route_onehot = route_ids[:, None] == jnp.arange(EXPERTS, dtype=jnp.int32)[None, :]
    gate_vals = jnp.sum(router_probs * route_onehot.astype(jnp.float32), axis=1, keepdims=True)
    chosen = route_onehot & live_bool[:, None]
    before = (
        jnp.arange(row_count, dtype=jnp.int32)[:, None]
        >= jnp.arange(row_count, dtype=jnp.int32)[None, :]
    ).astype(low_type)
    counts = matmul(before, chosen.astype(low_type)).astype(jnp.int32)
    rank_in = jnp.sum(jnp.where(chosen, counts - 1, 0), axis=1)
    slot_ids = jnp.where(live_bool, route_ids * capacity + rank_in, -1)
    slot_of = jnp.arange(dp_count * capacity, dtype=jnp.int32)
    slot_of = (slot_of // (capacity * split_count)) * capacity + slot_of % capacity
    dispatch = (slot_of[:, None] == slot_ids[None, :]).astype(low_type)

    grad_out = cotangent.astype(jnp.float32)
    grad_expert = (gate_vals * row_live * grad_out).astype(low_type)
    sent = matmul(dispatch, jnp.concatenate([h_two, grad_expert], axis=1)).astype(low_type)
    (got,) = exchange(
        3, (("dp", "swap", 0),), sent.reshape(dp_count, capacity, 2 * model_width)
    )
    got = got.reshape(dp_count * capacity, 2 * model_width)
    back = expert_rows_both_ways(got, w_in, w_out)
    returned, got_all = exchange(
        4,
        (("dp", "swap", 0), ("rep", spread_kind, 1)),
        back.reshape(dp_count, capacity, 2 * model_width),
        got,
    )
    landed = dot_over(dispatch, returned.reshape(dp_count * capacity, 2 * model_width), 0, 0)
    expert_rows, grad_h_two = landed[:, :model_width], landed[:, model_width:]

    block_out = x_one + gate_vals * expert_rows * row_live
    grad_gate = jnp.sum(grad_out * expert_rows, axis=1, keepdims=True) * row_live
    grad_probs = route_onehot.astype(jnp.float32) * grad_gate
    grad_logits = router_probs * (
        grad_probs - jnp.sum(router_probs * grad_probs, axis=1, keepdims=True)
    )
    grad_router = jnp.dot(h_two.astype(jnp.float32).T, grad_logits, precision=HIGH)
    grad_h_two = grad_h_two + jnp.dot(
        grad_logits, router_full.astype(jnp.float32).T, precision=HIGH
    )
    _, norm_two_pull = jax.vjp(rms_scale, x_one, gain_second)
    grad_x_norm, grad_gain_two = norm_two_pull(grad_h_two)
    grad_x_one = grad_out + grad_x_norm
    grad_branch = (grad_x_one * row_live).astype(low_type)

    (branch_all,) = exchange(5, (("rep", spread_kind, 0),), grad_branch)
    grad_branch_group = branch_all.reshape(group_rows, model_width)
    grad_w_output = dot_over(mixture, grad_branch_group, 0, 0).astype(low_type)
    dmix = dot_over(grad_branch_group, w_out_rows, 1, 1).astype(low_type)
    dqkv, dline = attend_back(qkv, dmix, probs, heads, row_count)
    grad_table = jnp.dot(dline, bucket_hot.T, precision=HIGH)
    grad_w_qkv = dot_over(h_one, dqkv, 0, 0).astype(low_type)
    grad_h_parts = dot_over(dqkv, w_qkv, 1, 1).astype(low_type)
    grad_h_got, grad_out_cols = exchange(
        6,
        (("rep", "swap", 0), ("rep", "swap", 1)),
        grad_h_parts.reshape(rep_count, row_count, model_width),
        grad_w_output.reshape(width, rep_count, width).transpose(1, 0, 2),
    )
    grad_h_one = jnp.sum(grad_h_got.astype(jnp.float32), axis=0)
    _, norm_one_pull = jax.vjp(rms_scale, x_in, gain_first)
    grad_x_in, grad_gain_one = norm_one_pull(grad_h_one)
    grad_input = grad_x_one + grad_x_in

    table_whole = lax.dynamic_update_slice_in_dim(
        jnp.zeros((HEADS, BUCKETS), jnp.float32), grad_table, rep_at * heads, 0
    )
    small_grads = packed(
        [
            x.reshape(dp_count, -1)
            for x in (grad_gain_one, grad_gain_two, table_whole, grad_router)
        ],
        (dp_count,),
    )
    weight_all, small_all, grad_w_in, grad_w_out = closing(
        7,
        jnp.concatenate(
            [
                grad_w_qkv.reshape(dp_count, shard, 3 * width),
                grad_out_cols.reshape(dp_count, shard, width),
            ],
            axis=2,
        ),
        small_grads,
        got_all.reshape(-1, 2 * model_width),
        w_in,
        w_out,
    )
    weights = (
        weight_all.reshape(rep_count, shard, 4, width)
        .transpose(2, 1, 0, 3)
        .reshape(4, shard, model_width)
        .astype(jnp.float32)
    )
    small_sum = jnp.sum(small_all, axis=0).reshape(-1)
    out_gain_one, out_gain_two, out_table, out_router = unpacked(small_sum, small_widths)

    return (
        block_out.astype(low_type),
        grad_input,
        out_gain_one,
        weights[0],
        weights[1],
        weights[2],
        weights[3],
        out_table,
        out_gain_two,
        out_router.reshape(shard, EXPERTS),
        grad_w_in.astype(jnp.float32),
        grad_w_out.astype(jnp.float32),
    )


def solution(mesh):
    placed = (
        P(("dp", "rep"), None),
        P("dp", None),
        P(),
        P(("dp", "rep"), None),
        P("dp"),
        P("dp", None),
        P("dp", None),
        P("dp", None),
        P("dp", None),
        P("dp"),
        P("dp"),
        P("dp", None),
        P(None, "dp"),
        P("dp", None),
        P(("dp", "rep"), None),
    )
    return jax.shard_map(
        on_device,
        mesh=mesh,
        in_specs=placed,
        out_specs=(
            P(("dp", "rep"), None),
            P(("dp", "rep"), None),
            P("dp"),
            P("dp", None),
            P("dp", None),
            P("dp", None),
            P("dp", None),
            P("dp"),
            P("dp"),
            P("dp", None),
            P(None, "dp"),
            P("dp", None),
        ),
        check_vma=False,
    )
```
